32 devices in a mesh: prow: 8 (over y, x, core), pcol: 4 (over z).
Axes of the slice: x: 2, y: 2, z: 4, core: 2. Of those that a mesh axis runs over, the one named last changes fastest.
Arguments:
- designs: float32 [8192, 64], P('prow'), may hold values from -4 to 4
- length_weights: float32 [64], replicated, may hold values from 0.002 to 0.03
- trailing: float32 [16384, 16384], P('prow', 'pcol'), as said below
Outputs:
- updated_trailing: float32 [16384, 16384], P('prow', 'pcol')
- panel_rows: float32 [16384, 512], P('prow', 'pcol')
- panel_factor: float32 [512, 512], P(None, 'pcol')
The draws below stay inside these ranges and needn't reach their ends.
Inputs may be any that keep to these rules, and one draw needn't show every extreme that they name: `trailing`: symmetric.
All inputs are finite; a program needn't handle non-finite values.
Results may differ from the reference program's by a relative error of at most 0.0003.
Values sent between devices are 32-bit elements; how exact they have to be, the bound alone decides.
A program may use at most 192 MiB of HBM per device.

```python
import math
import jax
import jax.numpy as jnp
from jax import lax

DIM = 64
PANEL = 512
DESIGNS = 8192
TRAIL = 16384


def draw_trailing(key, part):
    noise_key = jax.random.fold_in(key, 11)
    diag_key = jax.random.fold_in(key, 12)
    noise = jnp.clip(jax.random.normal(noise_key, (TRAIL, TRAIL), jnp.float32), -6.0, 6.0)
    symmetric = (noise + noise.T) * 0.15
    diagonal = jax.random.uniform(diag_key, (TRAIL,), jnp.float32, 1.0, 4.0)
    return symmetric + jnp.diag(diagonal)


def shard_levels(own_key, extent, cuts, low, high):
    factor_of, own = 1.0, jax.random.fold_in(own_key, 6)
    for axis_at, shards_of in cuts:
        steps = jnp.exp(jax.random.uniform(jax.random.fold_in(own, axis_at), (shards_of,), jnp.float32, low / len(cuts), high / len(cuts)))
        factor_of = factor_of * jnp.repeat(steps, extent[axis_at] // shards_of).reshape([-1 if axis == axis_at else 1 for axis in range(len(extent))])
    return factor_of


def normal_values(key, dims, spread, limit, shards=(), kind=jnp.bfloat16):
    result = spread * jax.random.normal(key, dims, jnp.float32)
    if shards:
        result = result * shard_levels(key, dims, shards, -0.22, 0.18)
    return jnp.clip(result, -limit, limit).astype(kind)


def setup_inputs(seed: int = 0) -> dict:
    key_of = jax.random.split(jax.random.key(seed), 4)
    return {
        "designs": normal_values(key_of[0], (DESIGNS, DIM), 1.0, 4.0, ((0, 8),), jnp.float32),
        "length_weights": jnp.clip(jnp.exp(jax.random.uniform(key_of[1], (DIM,), jnp.float32, math.log(0.002), math.log(0.03))), 0.002, 0.03),
        "trailing": draw_trailing(jax.random.fold_in(key_of[3], 71), 0),
    }


signal_variance = 4.0
nugget_level = 0.1

def scaled_pair(row_points, panel_points, length_weights):
    root_weights = jnp.sqrt(length_weights)
    return (row_points * root_weights, panel_points * root_weights)

def kernel_values(scaled_rows, scaled_panel):
    inner_terms = jnp.dot(scaled_rows, scaled_panel.T, precision=lax.Precision.HIGHEST)
    squares_rows = lax.optimization_barrier(jnp.sum(scaled_rows * scaled_rows, axis=1))[:, None]
    squares_panel = lax.optimization_barrier(jnp.sum(scaled_panel * scaled_panel, axis=1))[None, :]
    return signal_variance * jnp.exp(-(squares_rows + squares_panel - 2.0 * inner_terms))

def cross_block(row_points, panel_points, length_weights):
    scaled_rows, scaled_panel = scaled_pair(row_points, panel_points, length_weights)
    kernel = kernel_values(scaled_rows, scaled_panel)
    panel_gap = scaled_rows[:, -2][:, None] - scaled_panel[:, -2][None, :]
    trail_gap = scaled_rows[:, -1][:, None] - scaled_panel[:, -1][None, :]
    derivative_rows = -2.0 * kernel * trail_gap * panel_gap
    value_rows = math.sqrt(2.0) * kernel * panel_gap
    stacked = jnp.stack([derivative_rows, value_rows], axis=1)
    return stacked.reshape(2 * row_points.shape[0], panel_points.shape[0])

def diagonal_block(row_points, panel_points, length_weights, offset):
    scaled_rows, scaled_panel = scaled_pair(row_points, panel_points, length_weights)
    kernel = kernel_values(scaled_rows, scaled_panel)
    panel_gap = scaled_rows[:, -2][:, None] - scaled_panel[:, -2][None, :]
    row_iota = lax.broadcasted_iota(jnp.int32, kernel.shape, 0)
    col_iota = lax.broadcasted_iota(jnp.int32, kernel.shape, 1) + offset
    return kernel * (1.0 - 2.0 * panel_gap * panel_gap) + jnp.where(row_iota == col_iota, nugget_level, 0.0)

def reference(designs, length_weights, trailing):
    panel_points = designs[DESIGNS - PANEL:]
    block = diagonal_block(panel_points, panel_points, length_weights, 0)
    panel_factor = jnp.linalg.cholesky(block)
    cross = cross_block(designs, panel_points, length_weights)
    panel_rows = jax.scipy.linalg.solve_triangular(panel_factor, cross.T, lower=True).T
    updated = trailing - jnp.dot(panel_rows, panel_rows.T, precision=lax.Precision.HIGHEST)
    return (updated, panel_rows, panel_factor)
```

```python
import functools
import math

import jax
import jax.numpy as jnp
from jax import lax
from jax.experimental import pallas as pl
from jax.experimental.pallas import tpu as pltpu
from jax.sharding import PartitionSpec as P

PANEL = 512
BLOCK = 128
GROUP = 16
MESH = pl.DeviceIdType.MESH
BF16 = jnp.bfloat16
F32 = jnp.float32
HIGHEST = lax.Precision.HIGHEST

signal_variance = 4.0
nugget_level = 0.1


def split2(x):
    high = x.astype(BF16)
    return high, (x - high.astype(F32)).astype(BF16)


def split3(x):
    high = x.astype(BF16)
    rest = x - high.astype(F32)
    mid = rest.astype(BF16)
    return high, mid, (rest - mid.astype(F32)).astype(BF16)


def dot_tn(a, b, precision=None):
    return lax.dot_general(
        a, b, (((0,), (0,)), ((), ())), precision=precision, preferred_element_type=F32
    )


def dot_nt(a, b):
    return lax.dot_general(a, b, (((1,), (1,)), ((), ())), preferred_element_type=F32)


def gather_kernel(grid_rows, grid_cols, own, panel, cols, send_sem, local_sem, panel_sem, cols_sem):
    me = lax.axis_index("prow")
    col = lax.axis_index("pcol")
    per = own.shape[1]
    panel_width = min(per, PANEL)
    holders = PANEL // panel_width
    share = grid_rows // grid_cols
    barrier = pltpu.get_barrier_semaphore()
    for step in range(1, grid_rows):
        peer = lax.rem(me + step, grid_rows)
        pl.semaphore_signal(barrier, inc=1, device_id=(peer, col), device_id_type=MESH)
    pl.semaphore_wait(barrier, grid_rows - 1)

    pieces = []
    for at in range(holders):
        source = own.at[:, per - panel_width :] if panel_width < per else own
        target = panel.at[:, at * panel_width : (at + 1) * panel_width]
        pieces.append((grid_rows - holders + at, source, target, panel_sem.at[at], at))
    for at in range(share):
        target = cols.at[:, at * per : (at + 1) * per]
        pieces.append((col * share + at, own, target, cols_sem.at[at], holders + at))

    def remote(piece, step):
        _, source, target, sem, at = piece
        peer = lax.rem(me + step, grid_rows)
        return pltpu.make_async_remote_copy(
            src_ref=source,
            dst_ref=target,
            send_sem=send_sem.at[at, step - 1],
            recv_sem=sem,
            device_id=(peer, col),
            device_id_type=MESH,
        )

    for piece in pieces:
        holder, source, target, sem, at = piece

        @pl.when(me == holder)
        def _():
            for step in range(1, grid_rows):
                remote(piece, step).start()
            pltpu.make_async_copy(source, target, local_sem.at[at]).start()

    for piece in pieces:
        holder, source, target, sem, at = piece

        @pl.when(me == holder)
        def _():
            for step in range(1, grid_rows):
                remote(piece, step).wait_send()
            pltpu.make_async_copy(source, target, local_sem.at[at]).wait()

        @pl.when(me != holder)
        def _():
            remote(piece, 1).wait_recv()


def gather_designs(own, grid_rows, grid_cols):
    variables, per = own.shape
    holders = PANEL // min(per, PANEL)
    share = grid_rows // grid_cols
    return pl.pallas_call(
        functools.partial(gather_kernel, grid_rows, grid_cols),
        out_shape=(
            jax.ShapeDtypeStruct((variables, PANEL), F32),
            jax.ShapeDtypeStruct((variables, per * share), F32),
        ),
        in_specs=[pl.BlockSpec(memory_space=pltpu.VMEM)],
        out_specs=(pl.BlockSpec(memory_space=pltpu.VMEM), pl.BlockSpec(memory_space=pltpu.VMEM)),
        scratch_shapes=[
            pltpu.SemaphoreType.DMA((holders + share, grid_rows - 1)),
            pltpu.SemaphoreType.DMA((holders + share,)),
            pltpu.SemaphoreType.DMA((holders,)),
            pltpu.SemaphoreType.DMA((share,)),
        ],
        compiler_params=pltpu.CompilerParams(collective_id=0, has_side_effects=True),
        name="gather_designs",
    )(own)


def factor_block(work):
    row_iota = lax.broadcasted_iota(jnp.int32, (GROUP, BLOCK), 0)
    for first in range(0, BLOCK, GROUP):
        rows = work[first : first + GROUP, :]
        left, right = rows[:, :BLOCK], rows[:, BLOCK:]
        columns = [
            jnp.broadcast_to(left[:, first + k : first + k + 1], (GROUP, BLOCK))
            for k in range(GROUP)
        ]
        scales = jnp.zeros((GROUP, BLOCK), F32)
        for k in range(GROUP):
            root = lax.rsqrt(columns[k][k : k + 1, :])
            inverse = root * root
            scales = jnp.where(row_iota == k, root, scales)
            below = jnp.where(row_iota > k, columns[k], 0.0)
            for m in range(k + 1, GROUP):
                columns[m] = columns[m] - (below * columns[m][k : k + 1, :]) * inverse
            left = left - below * (left[k : k + 1, :] * inverse)
            right = right - below * (right[k : k + 1, :] * inverse)
        left, right = left * scales, right * scales
        work[first : first + GROUP, :BLOCK] = left
        work[first : first + GROUP, BLOCK:] = right
        last = first + GROUP
        if last < BLOCK:
            high, mid, low = split3(jnp.concatenate([left, right], 1))
            a = jnp.concatenate([high, high, mid, high, mid, low], 0)[:, :BLOCK]
            b = jnp.concatenate([high, mid, high, low, mid, high], 0)
            work[last:, :] = work[last:, :] - dot_tn(a, b)[last:, :]


def factor_kernel(panel, root_weights, inverse, factor, matrix, upper, work):
    width = factor.shape[1]
    scaled = panel[...] * root_weights[...]
    flipped = scaled.T
    inner = dot_tn(scaled, scaled, HIGHEST)
    squares = jnp.sum(scaled * scaled, axis=0, keepdims=True)
    squares_col = jnp.sum(flipped * flipped, axis=1, keepdims=True)
    kernel = signal_variance * jnp.exp(-(squares_col + squares - 2.0 * inner))
    gap = flipped[:, -2:-1] - scaled[-2:-1, :]
    row_iota = lax.broadcasted_iota(jnp.int32, (PANEL, PANEL), 0)
    col_iota = lax.broadcasted_iota(jnp.int32, (PANEL, PANEL), 1)
    matrix[...] = kernel * (1.0 - 2.0 * gap * gap) + jnp.where(
        row_iota == col_iota, nugget_level, 0.0
    )
    upper[...] = jnp.zeros_like(upper)
    work_row = lax.broadcasted_iota(jnp.int32, (BLOCK, BLOCK), 0)
    work_col = lax.broadcasted_iota(jnp.int32, (BLOCK, BLOCK), 1)
    identity = jnp.where(work_row == work_col, 1.0, 0.0)
    blocks = PANEL // BLOCK

    @pl.loop(0, blocks)
    def _(at):
        offset = pl.multiple_of(at * BLOCK, BLOCK)
        work[:, :BLOCK] = matrix[pl.ds(offset, BLOCK), pl.ds(offset, BLOCK)]
        work[:, BLOCK:] = identity
        factor_block(work)
        part_upper = jnp.where(work_col >= work_row, work[:, :BLOCK], 0.0)
        part_inverse = jnp.where(work_col <= work_row, work[:, BLOCK:], 0.0)
        for k in range(blocks):

            @pl.when(at == k)
            def _():
                low, high = k * BLOCK, (k + 1) * BLOCK
                solved = jnp.dot(
                    part_inverse,
                    matrix[low:high, :],
                    precision=HIGHEST,
                    preferred_element_type=F32,
                )
                pieces = [part_inverse]
                if k > 0:
                    pieces.insert(0, solved[:, :low])
                if high < PANEL:
                    pieces.append(solved[:, high:])
                    upper[low:high, high:] = solved[:, high:]
                upper[low:high, low:high] = part_upper
                whole = jnp.concatenate(pieces, 1)
                matrix[low:high, :] = whole
                if high < PANEL:
                    matrix[high:, low:high] = jnp.zeros((PANEL - high, BLOCK), F32)
                    matrix[high:, :] = matrix[high:, :] - dot_tn(
                        solved[:, high:], whole, HIGHEST
                    )

    inverse[...] = jnp.where(col_iota <= row_iota, matrix[...], 0.0)
    col = lax.axis_index("pcol")
    first = pl.multiple_of(col * width, width)
    factor[...] = upper[pl.ds(first, width), :].T


def factor_panel(panel, root_weights, width):
    return pl.pallas_call(
        factor_kernel,
        out_shape=(
            jax.ShapeDtypeStruct((PANEL, PANEL), F32),
            jax.ShapeDtypeStruct((PANEL, width), F32),
        ),
        in_specs=[pl.BlockSpec(memory_space=pltpu.VMEM)] * 2,
        out_specs=(pl.BlockSpec(memory_space=pltpu.VMEM), pl.BlockSpec(memory_space=pltpu.VMEM)),
        scratch_shapes=[
            pltpu.VMEM((PANEL, PANEL), F32),
            pltpu.VMEM((PANEL, PANEL), F32),
            pltpu.VMEM((BLOCK, 2 * BLOCK), F32),
        ],
        compiler_params=pltpu.CompilerParams(vmem_limit_bytes=32 * 2**20),
        name="factor_panel",
    )(panel, root_weights)


CHUNK = 128


def update_kernel(
    rows, cols, panel, weights_row, weights_col, inverse, trailing,
    updated, shard,
    panel_parts, panel_rows, inverse_parts, cross, row_parts, col_parts,
):
    i, j = pl.program_id(0), pl.program_id(1)
    width = shard.shape[1]
    tile_m, tile_n = trailing.shape
    half = PANEL // 2

    @pl.when((i == 0) & (j == 0))
    def _():
        scaled = panel[...] * weights_col[...]
        high, mid = split2(scaled)
        panel_parts[...] = jnp.concatenate([high, mid, high, mid], 0)
        panel_rows[0:1, :] = jnp.sum(scaled * scaled, axis=0, keepdims=True)
        panel_rows[1:2, :] = scaled[-2:-1, :]
        panel_rows[2:3, :] = scaled[-1:, :]
        high, low = split2(inverse[...])
        inverse_parts[...] = jnp.concatenate([high, low, high], 1)

    def factor_rows(points):
        scaled = points * weights_row[...]
        high, mid = split2(scaled)
        parts = jnp.concatenate([high, high, mid, mid], 1)
        inner = jnp.dot(parts, panel_parts[...], preferred_element_type=F32)
        squares = jnp.sum(scaled * scaled, axis=1, keepdims=True)
        kernel = jnp.exp(2.0 * inner - squares - panel_rows[0:1, :])
        value = (signal_variance * math.sqrt(2.0)) * kernel * (
            scaled[:, -2:-1] - panel_rows[1:2, :]
        )
        derivative = value * (math.sqrt(2.0) * (panel_rows[2:3, :] - scaled[:, -1:]))
        for lane in range(0, PANEL, 128):
            tile = cross.at[lane // 128]
            tile[pl.ds(0, CHUNK, stride=2), :] = derivative[:, lane : lane + 128]
            tile[pl.ds(1, CHUNK, stride=2), :] = value[:, lane : lane + 128]
        high, low = split2(jnp.concatenate([cross[at] for at in range(PANEL // 128)], 1))
        parts = jnp.concatenate([high, high, low], 1)
        left = jnp.concatenate([high[:, :half], high[:, :half], low[:, :half]], 1)
        left_inverse = jnp.concatenate(
            [inverse_parts[:half, part * PANEL : part * PANEL + half] for part in range(3)], 1
        )
        solved = jnp.concatenate(
            [dot_nt(left, left_inverse), dot_nt(parts, inverse_parts[half:, :])], 1
        )
        return parts, solved

    @pl.when(j == 0)
    def _():
        col = lax.axis_index("pcol")
        first = pl.multiple_of(col * width, width)

        @pl.loop(0, tile_m // (2 * CHUNK))
        def _(at):
            start = pl.multiple_of(at * CHUNK, CHUNK)
            parts, solved = factor_rows(rows[pl.ds(start, CHUNK), :])
            high, low = split2(solved)
            place = pl.ds(pl.multiple_of(at * 2 * CHUNK, 2 * CHUNK), 2 * CHUNK)
            row_parts[place, :] = jnp.concatenate([high, high, low], 1)
            shard[place, :] = dot_nt(parts, inverse_parts[pl.ds(first, width), :])

    @pl.when(i == 0)
    def _():
        @pl.loop(0, tile_n // (2 * CHUNK))
        def _(at):
            start = pl.multiple_of(at * CHUNK, CHUNK)
            _, solved = factor_rows(cols[pl.ds(start, CHUNK), :])
            high, low = split2(solved)
            place = pl.ds(pl.multiple_of(j * tile_n + at * 2 * CHUNK, 2 * CHUNK), 2 * CHUNK)
            col_parts[place, :] = jnp.concatenate([high, low, high], 1)

    @pl.loop(0, tile_n // 256)
    def _(at):
        lanes = pl.ds(pl.multiple_of(at * 256, 256), 256)
        place = pl.ds(pl.multiple_of(j * tile_n + at * 256, 256), 256)
        updated[:, lanes] = trailing[:, lanes] - dot_nt(row_parts[...], col_parts[place, :])


def update(designs, cols, panel, root_weights, inverse, trailing, width):
    height, extent = trailing.shape
    tile_m, tile_n = min(1024, height), min(1024, extent)
    variables = designs.shape[1]
    return pl.pallas_call(
        update_kernel,
        grid=(height // tile_m, extent // tile_n),
        out_shape=(
            jax.ShapeDtypeStruct((height, extent), F32),
            jax.ShapeDtypeStruct((height, width), F32),
        ),
        in_specs=[
            pl.BlockSpec((tile_m // 2, variables), lambda i, j: (i, 0)),
            pl.BlockSpec((tile_n // 2, variables), lambda i, j: (j, 0)),
            pl.BlockSpec((variables, PANEL), lambda i, j: (0, 0)),
            pl.BlockSpec((1, variables), lambda i, j: (0, 0)),
            pl.BlockSpec((variables, 1), lambda i, j: (0, 0)),
            pl.BlockSpec((PANEL, PANEL), lambda i, j: (0, 0)),
            pl.BlockSpec((tile_m, tile_n), lambda i, j: (i, j)),
        ],
        out_specs=(
            pl.BlockSpec((tile_m, tile_n), lambda i, j: (i, j)),
            pl.BlockSpec((tile_m, width), lambda i, j: (i, 0)),
        ),
        scratch_shapes=[
            pltpu.VMEM((4 * variables, PANEL), BF16),
            pltpu.VMEM((8, PANEL), F32),
            pltpu.VMEM((PANEL, 3 * PANEL), BF16),
            pltpu.VMEM((PANEL // 128, 2 * CHUNK, 128), F32),
            pltpu.VMEM((tile_m, 3 * PANEL), BF16),
            pltpu.VMEM((extent, 3 * PANEL), BF16),
        ],
        compiler_params=pltpu.CompilerParams(vmem_limit_bytes=56 * 2**20),
        name="update_trailing",
    )(designs, cols, panel, root_weights[None, :], root_weights[:, None], inverse, trailing)


def body(designs, length_weights, trailing):
    grid_rows = lax.axis_size("prow")
    grid_cols = lax.axis_size("pcol")
    width = PANEL // grid_cols
    root_weights = jnp.sqrt(length_weights)
    panel, cols = gather_designs(designs.T, grid_rows, grid_cols)
    inverse, factor = factor_panel(panel, root_weights[:, None], width)
    updated, shard = update(designs, cols.T, panel, root_weights, inverse, trailing, width)
    return updated, shard, factor


def solution(mesh):
    in_specs = (P("prow", None), P(), P("prow", "pcol"))
    out_specs = (P("prow", "pcol"), P("prow", "pcol"), P(None, "pcol"))
    return jax.shard_map(body, mesh=mesh, in_specs=in_specs, out_specs=out_specs, check_vma=False)
```

```python
import functools
import math

import jax
import jax.numpy as jnp
from jax import lax
from jax.experimental import pallas as pl
from jax.experimental.pallas import tpu as pltpu
from jax.sharding import PartitionSpec as P

PANEL = 512
BLOCK = 128
GROUP = 16
MESH = pl.DeviceIdType.MESH
BF16 = jnp.bfloat16
F32 = jnp.float32
HIGHEST = lax.Precision.HIGHEST

signal_variance = 4.0
nugget_level = 0.1


def split2(x):
    high = x.astype(BF16)
    return high, (x - high.astype(F32)).astype(BF16)


def split3(x):
    high = x.astype(BF16)
    rest = x - high.astype(F32)
    mid = rest.astype(BF16)
    return high, mid, (rest - mid.astype(F32)).astype(BF16)


def dot_tn(a, b, precision=None):
    return lax.dot_general(
        a, b, (((0,), (0,)), ((), ())), precision=precision, preferred_element_type=F32
    )


def dot_nt(a, b):
    return lax.dot_general(a, b, (((1,), (1,)), ((), ())), preferred_element_type=F32)


def gather_kernel(grid_rows, grid_cols, own, panel, cols, send_sem, local_sem, recv_sem):
    me = lax.axis_index("prow")
    col = lax.axis_index("pcol")
    chip, core = me // 2, lax.rem(me, 2)
    rounds = (grid_rows // 2).bit_length() - 1
    per = own.shape[1]
    panel_width = min(per, PANEL)
    holders = PANEL // panel_width
    share = grid_rows // grid_cols
    half = per // 2
    barrier = pltpu.get_barrier_semaphore()
    for step in range(1, grid_rows):
        peer = lax.rem(me + step, grid_rows)
        pl.semaphore_signal(barrier, inc=1, device_id=(peer, col), device_id_type=MESH)
    pl.semaphore_wait(barrier, grid_rows - 1)

    pieces = []
    for at in range(holders):
        source = own.at[:, per - panel_width :]
        target = panel.at[:, at * panel_width : (at + 1) * panel_width]
        pieces.append((grid_rows - holders + at, source, target))
    for part in range(2):
        for at in range(share):
            source = own.at[:, part * half : (part + 1) * half]
            start = at * per + part * half
            pieces.append((col * share + at, source, cols.at[:, start : start + half]))

    sibling = me + 1 - 2 * core
    plans = []
    for at, (holder, source, target) in enumerate(pieces):
        holder_chip, holder_core = holder // 2, lax.rem(holder, 2)
        order = list(range(rounds))
        if at % 2:
            order.reverse()
        differs = [
            lax.rem(chip // 2**bit + holder_chip // 2**bit, 2) == 1 for bit in order
        ]
        peers = [me + (1 - 2 * lax.rem(chip // 2**bit, 2)) * 2 ** (bit + 1) for bit in order]
        same = core == holder_core
        sends = []
        for step in range(rounds):
            wanted = same
            for later in range(step, rounds):
                wanted = wanted & jnp.logical_not(differs[later])
            sends.append((wanted, peers[step], step))
        sends.append((same, sibling, rounds))
        plans.append((at, me == holder, source, target, sends))

    def copy(at, source, target, peer, slot):
        return pltpu.make_async_remote_copy(
            src_ref=source,
            dst_ref=target,
            send_sem=send_sem.at[at, slot],
            recv_sem=recv_sem.at[at],
            device_id=(peer, col),
            device_id_type=MESH,
        )

    for at, holds, source, target, sends in plans:

        @pl.when(holds)
        def _():
            for _, peer, slot in sends:
                copy(at, source, target, peer, slot).start()
            pltpu.make_async_copy(source, target, local_sem.at[at]).start()

    for at, holds, source, target, sends in plans:

        @pl.when(jnp.logical_not(holds))
        def _():
            copy(at, source, target, sibling, 0).wait_recv()
            for wanted, peer, slot in sends:

                @pl.when(wanted)
                def _():
                    copy(at, target, target, peer, slot).start()

    for at, holds, source, target, sends in plans:

        @pl.when(holds)
        def _():
            pltpu.make_async_copy(source, target, local_sem.at[at]).wait()

        for wanted, peer, slot in sends:

            @pl.when(wanted)
            def _():
                copy(at, source, target, peer, slot).wait_send()


def gather_designs(own, grid_rows, grid_cols):
    variables, per = own.shape
    holders = PANEL // min(per, PANEL)
    share = grid_rows // grid_cols
    return pl.pallas_call(
        functools.partial(gather_kernel, grid_rows, grid_cols),
        out_shape=(
            jax.ShapeDtypeStruct((variables, PANEL), F32),
            jax.ShapeDtypeStruct((variables, per * share), F32),
        ),
        in_specs=[pl.BlockSpec(memory_space=pltpu.VMEM)],
        out_specs=(pl.BlockSpec(memory_space=pltpu.VMEM), pl.BlockSpec(memory_space=pltpu.VMEM)),
        scratch_shapes=[
            pltpu.SemaphoreType.DMA((holders + 2 * share, (grid_rows // 2).bit_length())),
            pltpu.SemaphoreType.DMA((holders + 2 * share,)),
            pltpu.SemaphoreType.DMA((holders + 2 * share,)),
        ],
        compiler_params=pltpu.CompilerParams(collective_id=0, has_side_effects=True),
        name="gather_designs",
    )(own)


def factor_block(work):
    row_iota = lax.broadcasted_iota(jnp.int32, (GROUP, BLOCK), 0)
    for first in range(0, BLOCK, GROUP):
        rows = work[first : first + GROUP, :]
        left, right = rows[:, :BLOCK], rows[:, BLOCK:]
        columns = [
            jnp.broadcast_to(left[:, first + k : first + k + 1], (GROUP, BLOCK))
            for k in range(GROUP)
        ]
        scales = jnp.zeros((GROUP, BLOCK), F32)
        for k in range(GROUP):
            root = lax.rsqrt(columns[k][k : k + 1, :])
            inverse = root * root
            scales = jnp.where(row_iota == k, root, scales)
            below = jnp.where(row_iota > k, columns[k], 0.0)
            for m in range(k + 1, GROUP):
                columns[m] = columns[m] - (below * columns[m][k : k + 1, :]) * inverse
            left = left - below * (left[k : k + 1, :] * inverse)
            right = right - below * (right[k : k + 1, :] * inverse)
        left, right = left * scales, right * scales
        work[first : first + GROUP, :BLOCK] = left
        work[first : first + GROUP, BLOCK:] = right
        last = first + GROUP
        if last < BLOCK:
            high, mid, low = split3(jnp.concatenate([left, right], 1))
            a = jnp.concatenate([high, high, mid, high, mid, low], 0)[:, :BLOCK]
            b = jnp.concatenate([high, mid, high, low, mid, high], 0)
            work[last:, :] = work[last:, :] - dot_tn(a, b)[last:, :]


def factor_kernel(panel, inverse, factor, matrix, upper, work):
    width = factor.shape[1]
    scaled = panel[...]
    flipped = scaled.T
    inner = dot_tn(scaled, scaled, HIGHEST)
    squares = jnp.sum(scaled * scaled, axis=0, keepdims=True)
    squares_col = jnp.sum(flipped * flipped, axis=1, keepdims=True)
    kernel = signal_variance * jnp.exp(-(squares_col + squares - 2.0 * inner))
    gap = flipped[:, -2:-1] - scaled[-2:-1, :]
    row_iota = lax.broadcasted_iota(jnp.int32, (PANEL, PANEL), 0)
    col_iota = lax.broadcasted_iota(jnp.int32, (PANEL, PANEL), 1)
    matrix[...] = kernel * (1.0 - 2.0 * gap * gap) + jnp.where(
        row_iota == col_iota, nugget_level, 0.0
    )
    upper[...] = jnp.zeros_like(upper)
    work_row = lax.broadcasted_iota(jnp.int32, (BLOCK, BLOCK), 0)
    work_col = lax.broadcasted_iota(jnp.int32, (BLOCK, BLOCK), 1)
    identity = jnp.where(work_row == work_col, 1.0, 0.0)
    blocks = PANEL // BLOCK

    @pl.loop(0, blocks)
    def _(at):
        offset = pl.multiple_of(at * BLOCK, BLOCK)
        work[:, :BLOCK] = matrix[pl.ds(offset, BLOCK), pl.ds(offset, BLOCK)]
        work[:, BLOCK:] = identity
        factor_block(work)
        part_upper = jnp.where(work_col >= work_row, work[:, :BLOCK], 0.0)
        part_inverse = jnp.where(work_col <= work_row, work[:, BLOCK:], 0.0)
        for k in range(blocks):

            @pl.when(at == k)
            def _():
                low, high = k * BLOCK, (k + 1) * BLOCK
                solved = jnp.dot(
                    part_inverse,
                    matrix[low:high, :],
                    precision=HIGHEST,
                    preferred_element_type=F32,
                )
                pieces = [part_inverse]
                if k > 0:
                    pieces.insert(0, solved[:, :low])
                if high < PANEL:
                    pieces.append(solved[:, high:])
                    upper[low:high, high:] = solved[:, high:]
                upper[low:high, low:high] = part_upper
                whole = jnp.concatenate(pieces, 1)
                matrix[low:high, :] = whole
                if high < PANEL:
                    matrix[high:, low:high] = jnp.zeros((PANEL - high, BLOCK), F32)
                    matrix[high:, :] = matrix[high:, :] - dot_tn(
                        solved[:, high:], whole, HIGHEST
                    )

    inverse[...] = jnp.where(col_iota <= row_iota, matrix[...], 0.0)
    col = lax.axis_index("pcol")
    first = pl.multiple_of(col * width, width)
    factor[...] = upper[pl.ds(first, width), :].T


def factor_panel(panel, width):
    return pl.pallas_call(
        factor_kernel,
        out_shape=(
            jax.ShapeDtypeStruct((PANEL, PANEL), F32),
            jax.ShapeDtypeStruct((PANEL, width), F32),
        ),
        in_specs=[pl.BlockSpec(memory_space=pltpu.VMEM)],
        out_specs=(pl.BlockSpec(memory_space=pltpu.VMEM), pl.BlockSpec(memory_space=pltpu.VMEM)),
        scratch_shapes=[
            pltpu.VMEM((PANEL, PANEL), F32),
            pltpu.VMEM((PANEL, PANEL), F32),
            pltpu.VMEM((BLOCK, 2 * BLOCK), F32),
        ],
        compiler_params=pltpu.CompilerParams(vmem_limit_bytes=32 * 2**20),
        name="factor_panel",
    )(panel)


CHUNK = 128


def update_kernel(
    rows, cols, panel, inverse, trailing,
    updated, shard,
    panel_parts, panel_rows, inverse_parts, cross, cross_next, row_parts, even_part, odd_part,
):
    step = pl.program_id(0)
    width = shard.shape[1]
    height = trailing.shape[0]
    half = PANEL // 2
    wide = 2 * CHUNK

    def cross_parts(points, stage):
        count = points.shape[1]
        scaled = points.T
        high, mid = split2(scaled)
        parts = jnp.concatenate([high, high, mid, mid], 1)
        inner = jnp.dot(parts, panel_parts[...], preferred_element_type=F32)
        squares = jnp.sum(scaled * scaled, axis=1, keepdims=True)
        kernel = jnp.exp(2.0 * inner - squares - panel_rows[0:1, :])
        value = (signal_variance * math.sqrt(2.0)) * kernel * (
            scaled[:, -2:-1] - panel_rows[1:2, :]
        )
        derivative = value * (math.sqrt(2.0) * (panel_rows[2:3, :] - scaled[:, -1:]))
        for lane in range(0, PANEL, 128):
            tile = stage.at[lane // 128]
            tile[pl.ds(0, count, stride=2), :] = derivative[:, lane : lane + 128]
            tile[pl.ds(1, count, stride=2), :] = value[:, lane : lane + 128]
        high, low = split2(jnp.concatenate([stage[at] for at in range(PANEL // 128)], 1))
        left = jnp.concatenate([high[:, :half], high[:, :half], low[:, :half]], 1)
        return left, jnp.concatenate([high, high, low], 1)

    def inverse_top():
        return jnp.concatenate(
            [inverse_parts[:half, part * PANEL : part * PANEL + half] for part in range(3)], 1
        )

    def make_columns(start, target):
        left, parts = cross_parts(cols[:, pl.ds(start, CHUNK)], cross_next)
        solved = jnp.concatenate(
            [dot_nt(inverse_top(), left), dot_nt(inverse_parts[half:, :], parts)], 0
        )
        high, low = split2(solved)
        target[:PANEL, :] = high
        target[PANEL : 2 * PANEL, :] = low
        target[2 * PANEL :, :] = high

    @pl.when(step == 0)
    def _():
        scaled = panel[...]
        high, mid = split2(scaled)
        panel_parts[...] = jnp.concatenate([high, mid, high, mid], 0)
        panel_rows[0:1, :] = jnp.sum(scaled * scaled, axis=0, keepdims=True)
        panel_rows[1:2, :] = scaled[-2:-1, :]
        panel_rows[2:3, :] = scaled[-1:, :]
        high, low = split2(inverse[...])
        inverse_parts[...] = jnp.concatenate([high, low, high], 1)
        col = lax.axis_index("pcol")
        first = pl.multiple_of(col * width, width)
        count = cross.shape[1] // 2

        @pl.loop(0, rows.shape[1] // count)
        def _(at):
            start = pl.multiple_of(at * count, count)
            left, parts = cross_parts(rows[:, pl.ds(start, count)], cross)
            solved = jnp.concatenate(
                [dot_nt(left, inverse_top()), dot_nt(parts, inverse_parts[half:, :])], 1
            )
            high, low = split2(solved)
            place = pl.ds(pl.multiple_of(at * 2 * count, 2 * count), 2 * count)
            row_parts[place, :] = jnp.concatenate([high, high, low], 1)
            shard[place, :] = dot_nt(parts, inverse_parts[pl.ds(first, width), :])

        make_columns(0, even_part)

    def subtract(lanes, part):
        for at in range(0, height, 512):
            updated[at : at + 512, lanes] = trailing[at : at + 512, lanes] - jnp.dot(
                row_parts[at : at + 512, :], part[...], preferred_element_type=F32
            )

    chunks = cols.shape[1] // CHUNK
    make_columns(pl.multiple_of((2 * step + 1) * CHUNK, CHUNK), odd_part)
    subtract(slice(0, wide), even_part)
    following = lax.rem(2 * step + 2, chunks)
    make_columns(pl.multiple_of(following * CHUNK, CHUNK), even_part)
    subtract(slice(wide, 2 * wide), odd_part)


def update(rows, cols, panel, inverse, trailing, width):
    height, extent = trailing.shape
    variables, count = rows.shape
    tile = 4 * CHUNK
    row_chunk = min(2 * CHUNK, count)
    return pl.pallas_call(
        update_kernel,
        grid=(extent // tile,),
        out_shape=(
            jax.ShapeDtypeStruct((height, extent), F32),
            jax.ShapeDtypeStruct((height, width), F32),
        ),
        in_specs=[
            pl.BlockSpec(rows.shape, lambda j: (0, 0)),
            pl.BlockSpec(cols.shape, lambda j: (0, 0)),
            pl.BlockSpec((variables, PANEL), lambda j: (0, 0)),
            pl.BlockSpec((PANEL, PANEL), lambda j: (0, 0)),
            pl.BlockSpec((height, tile), lambda j: (0, j)),
        ],
        out_specs=(
            pl.BlockSpec((height, tile), lambda j: (0, j)),
            pl.BlockSpec((height, width), lambda j: (0, 0)),
        ),
        scratch_shapes=[
            pltpu.VMEM((4 * variables, PANEL), BF16),
            pltpu.VMEM((8, PANEL), F32),
            pltpu.VMEM((PANEL, 3 * PANEL), BF16),
            pltpu.VMEM((PANEL // 128, 2 * row_chunk, 128), F32),
            pltpu.VMEM((PANEL // 128, 2 * CHUNK, 128), F32),
            pltpu.VMEM((height, 3 * PANEL), BF16),
            pltpu.VMEM((3 * PANEL, 2 * CHUNK), BF16),
            pltpu.VMEM((3 * PANEL, 2 * CHUNK), BF16),
        ],
        compiler_params=pltpu.CompilerParams(vmem_limit_bytes=44 * 2**20),
        name="update_trailing",
    )(rows, cols, panel, inverse, trailing)


def body(designs, length_weights, trailing):
    grid_rows = lax.axis_size("prow")
    grid_cols = lax.axis_size("pcol")
    width = PANEL // grid_cols
    scaled = designs.T * jnp.sqrt(length_weights)[:, None]
    panel, cols = gather_designs(scaled, grid_rows, grid_cols)
    inverse, factor = factor_panel(panel, width)
    updated, shard = update(scaled, cols, panel, inverse, trailing, width)
    return updated, shard, factor


def solution(mesh):
    in_specs = (P("prow", None), P(), P("prow", "pcol"))
    out_specs = (P("prow", "pcol"), P("prow", "pcol"), P(None, "pcol"))
    return jax.shard_map(body, mesh=mesh, in_specs=in_specs, out_specs=out_specs, check_vma=False)
```

```python
import functools
import math

import jax
import jax.numpy as jnp
from jax import lax
from jax.experimental import pallas as pl
from jax.experimental.pallas import tpu as pltpu
from jax.sharding import PartitionSpec as P

PANEL = 512
BLOCK = 128
GROUP = 16
MESH = pl.DeviceIdType.MESH
BF16 = jnp.bfloat16
F32 = jnp.float32
HIGHEST = lax.Precision.HIGHEST

signal_variance = 4.0
nugget_level = 0.1


def split2(x):
    high = x.astype(BF16)
    return high, (x - high.astype(F32)).astype(BF16)


def split3(x):
    high = x.astype(BF16)
    rest = x - high.astype(F32)
    mid = rest.astype(BF16)
    return high, mid, (rest - mid.astype(F32)).astype(BF16)


def dot_tn(a, b, precision=None):
    return lax.dot_general(
        a, b, (((0,), (0,)), ((), ())), precision=precision, preferred_element_type=F32
    )


def dot_nt(a, b):
    return lax.dot_general(a, b, (((1,), (1,)), ((), ())), preferred_element_type=F32)


def gather_kernel(grid_rows, grid_cols, own, panel, cols, send_sem, local_sem, recv_sem):
    me = lax.axis_index("prow")
    col = lax.axis_index("pcol")
    chip, core = me // 2, lax.rem(me, 2)
    rounds = (grid_rows // 2).bit_length() - 1
    per = own.shape[1]
    panel_width = min(per, PANEL)
    holders = PANEL // panel_width
    share = grid_rows // grid_cols
    half = per // 2
    barrier = pltpu.get_barrier_semaphore()
    for step in range(1, grid_rows):
        peer = lax.rem(me + step, grid_rows)
        pl.semaphore_signal(barrier, inc=1, device_id=(peer, col), device_id_type=MESH)
    pl.semaphore_wait(barrier, grid_rows - 1)

    pieces = []
    for at in range(holders):
        source = own.at[:, per - panel_width :]
        target = panel.at[:, at * panel_width : (at + 1) * panel_width]
        pieces.append((grid_rows - holders + at, source, target))
    for part in range(2):
        for at in range(share):
            source = own.at[:, part * half : (part + 1) * half]
            start = at * per + part * half
            pieces.append((col * share + at, source, cols.at[:, start : start + half]))

    sibling = me + 1 - 2 * core
    plans = []
    for at, (holder, source, target) in enumerate(pieces):
        holder_chip, holder_core = holder // 2, lax.rem(holder, 2)
        order = list(range(rounds))
        if at % 2:
            order.reverse()
        differs = [
            lax.rem(chip // 2**bit + holder_chip // 2**bit, 2) == 1 for bit in order
        ]
        peers = [me + (1 - 2 * lax.rem(chip // 2**bit, 2)) * 2 ** (bit + 1) for bit in order]
        same = core == holder_core
        sends = []
        for step in range(rounds):
            wanted = same
            for later in range(step, rounds):
                wanted = wanted & jnp.logical_not(differs[later])
            sends.append((wanted, peers[step], step))
        sends.append((same, sibling, rounds))
        plans.append((at, me == holder, source, target, sends))

    def copy(at, source, target, peer, slot):
        return pltpu.make_async_remote_copy(
            src_ref=source,
            dst_ref=target,
            send_sem=send_sem.at[at, slot],
            recv_sem=recv_sem.at[at],
            device_id=(peer, col),
            device_id_type=MESH,
        )

    for at, holds, source, target, sends in plans:

        @pl.when(holds)
        def _():
            for _, peer, slot in sends:
                copy(at, source, target, peer, slot).start()
            pltpu.make_async_copy(source, target, local_sem.at[at]).start()

    for at, holds, source, target, sends in plans:

        @pl.when(jnp.logical_not(holds))
        def _():
            copy(at, source, target, sibling, 0).wait_recv()
            for wanted, peer, slot in sends:

                @pl.when(wanted)
                def _():
                    copy(at, target, target, peer, slot).start()

    for at, holds, source, target, sends in plans:

        @pl.when(holds)
        def _():
            pltpu.make_async_copy(source, target, local_sem.at[at]).wait()

        for wanted, peer, slot in sends:

            @pl.when(wanted)
            def _():
                copy(at, source, target, peer, slot).wait_send()


def gather_designs(own, grid_rows, grid_cols):
    variables, per = own.shape
    holders = PANEL // min(per, PANEL)
    share = grid_rows // grid_cols
    return pl.pallas_call(
        functools.partial(gather_kernel, grid_rows, grid_cols),
        out_shape=(
            jax.ShapeDtypeStruct((variables, PANEL), F32),
            jax.ShapeDtypeStruct((variables, per * share), F32),
        ),
        in_specs=[pl.BlockSpec(memory_space=pltpu.VMEM)],
        out_specs=(pl.BlockSpec(memory_space=pltpu.VMEM), pl.BlockSpec(memory_space=pltpu.VMEM)),
        scratch_shapes=[
            pltpu.SemaphoreType.DMA((holders + 2 * share, (grid_rows // 2).bit_length())),
            pltpu.SemaphoreType.DMA((holders + 2 * share,)),
            pltpu.SemaphoreType.DMA((holders + 2 * share,)),
        ],
        compiler_params=pltpu.CompilerParams(
            collective_id=0, has_side_effects=True, vmem_limit_bytes=8 * 2**20
        ),
        name="gather_designs",
    )(own)


def factor_block(work):
    row_iota = lax.broadcasted_iota(jnp.int32, (GROUP, BLOCK), 0)
    for first in range(0, BLOCK, GROUP):
        rows = work[first : first + GROUP, :]
        left, right = rows[:, :BLOCK], rows[:, BLOCK:]
        columns = [
            jnp.broadcast_to(left[:, first + k : first + k + 1], (GROUP, BLOCK))
            for k in range(GROUP)
        ]
        scales = jnp.zeros((GROUP, BLOCK), F32)
        for k in range(GROUP):
            root = lax.rsqrt(columns[k][k : k + 1, :])
            inverse = root * root
            scales = jnp.where(row_iota == k, root, scales)
            below = jnp.where(row_iota > k, columns[k], 0.0)
            for m in range(k + 1, GROUP):
                columns[m] = columns[m] - (below * columns[m][k : k + 1, :]) * inverse
            left = left - below * (left[k : k + 1, :] * inverse)
            right = right - below * (right[k : k + 1, :] * inverse)
        left, right = left * scales, right * scales
        work[first : first + GROUP, :BLOCK] = left
        work[first : first + GROUP, BLOCK:] = right
        last = first + GROUP
        if last < BLOCK:
            high, mid, low = split3(jnp.concatenate([left, right], 1))
            a = jnp.concatenate([high, high, mid, high, mid, low], 0)[:, :BLOCK]
            b = jnp.concatenate([high, mid, high, low, mid, high], 0)
            work[last:, :] = work[last:, :] - dot_tn(a, b)[last:, :]


def factor_kernel(panel, inverse, factor, matrix, upper, work):
    width = factor.shape[1]
    scaled = panel[...]
    flipped = scaled.T
    inner = dot_tn(scaled, scaled, HIGHEST)
    squares = jnp.sum(scaled * scaled, axis=0, keepdims=True)
    squares_col = jnp.sum(flipped * flipped, axis=1, keepdims=True)
    kernel = signal_variance * jnp.exp(-(squares_col + squares - 2.0 * inner))
    gap = flipped[:, -2:-1] - scaled[-2:-1, :]
    row_iota = lax.broadcasted_iota(jnp.int32, (PANEL, PANEL), 0)
    col_iota = lax.broadcasted_iota(jnp.int32, (PANEL, PANEL), 1)
    matrix[...] = kernel * (1.0 - 2.0 * gap * gap) + jnp.where(
        row_iota == col_iota, nugget_level, 0.0
    )
    upper[...] = jnp.zeros_like(upper)
    work_row = lax.broadcasted_iota(jnp.int32, (BLOCK, BLOCK), 0)
    work_col = lax.broadcasted_iota(jnp.int32, (BLOCK, BLOCK), 1)
    identity = jnp.where(work_row == work_col, 1.0, 0.0)
    blocks = PANEL // BLOCK

    @pl.loop(0, blocks)
    def _(at):
        offset = pl.multiple_of(at * BLOCK, BLOCK)
        work[:, :BLOCK] = matrix[pl.ds(offset, BLOCK), pl.ds(offset, BLOCK)]
        work[:, BLOCK:] = identity
        factor_block(work)
        part_upper = jnp.where(work_col >= work_row, work[:, :BLOCK], 0.0)
        part_inverse = jnp.where(work_col <= work_row, work[:, BLOCK:], 0.0)
        for k in range(blocks):

            @pl.when(at == k)
            def _():
                low, high = k * BLOCK, (k + 1) * BLOCK
                solved = jnp.dot(
                    part_inverse,
                    matrix[low:high, :],
                    precision=HIGHEST,
                    preferred_element_type=F32,
                )
                pieces = [part_inverse]
                if k > 0:
                    pieces.insert(0, solved[:, :low])
                if high < PANEL:
                    pieces.append(solved[:, high:])
                    upper[low:high, high:] = solved[:, high:]
                upper[low:high, low:high] = part_upper
                whole = jnp.concatenate(pieces, 1)
                matrix[low:high, :] = whole
                if high < PANEL:
                    matrix[high:, low:high] = jnp.zeros((PANEL - high, BLOCK), F32)
                    matrix[high:, :] = matrix[high:, :] - dot_tn(
                        solved[:, high:], whole, HIGHEST
                    )

    inverse[...] = jnp.where(col_iota <= row_iota, matrix[...], 0.0)
    col = lax.axis_index("pcol")
    first = pl.multiple_of(col * width, width)
    factor[...] = upper[pl.ds(first, width), :].T


def factor_panel(panel, width):
    return pl.pallas_call(
        factor_kernel,
        out_shape=(
            jax.ShapeDtypeStruct((PANEL, PANEL), F32),
            jax.ShapeDtypeStruct((PANEL, width), F32),
        ),
        in_specs=[pl.BlockSpec(memory_space=pltpu.VMEM)],
        out_specs=(pl.BlockSpec(memory_space=pltpu.VMEM), pl.BlockSpec(memory_space=pltpu.VMEM)),
        scratch_shapes=[
            pltpu.VMEM((PANEL, PANEL), F32),
            pltpu.VMEM((PANEL, PANEL), F32),
            pltpu.VMEM((BLOCK, 2 * BLOCK), F32),
        ],
        compiler_params=pltpu.CompilerParams(vmem_limit_bytes=16 * 2**20),
        name="factor_panel",
    )(panel)


CHUNK = 128


def update_kernel(
    rows, cols, panel, inverse, trailing,
    updated, shard,
    panel_parts, panel_rows, inverse_parts, cross, cross_next, row_parts, even_part, odd_part,
):
    step = pl.program_id(0)
    width = shard.shape[1]
    height = trailing.shape[0]
    half = PANEL // 2
    wide = 2 * CHUNK

    def cross_parts(points, stage):
        count = points.shape[1]
        scaled = points.T
        high, mid = split2(scaled)
        parts = jnp.concatenate([high, high, mid, mid], 1)
        inner = jnp.dot(parts, panel_parts[...], preferred_element_type=F32)
        squares = jnp.sum(scaled * scaled, axis=1, keepdims=True)
        kernel = jnp.exp(2.0 * inner - squares - panel_rows[0:1, :])
        value = (signal_variance * math.sqrt(2.0)) * kernel * (
            scaled[:, -2:-1] - panel_rows[1:2, :]
        )
        derivative = value * (math.sqrt(2.0) * (panel_rows[2:3, :] - scaled[:, -1:]))
        for lane in range(0, PANEL, 128):
            tile = stage.at[lane // 128]
            tile[pl.ds(0, count, stride=2), :] = derivative[:, lane : lane + 128]
            tile[pl.ds(1, count, stride=2), :] = value[:, lane : lane + 128]
        high, low = split2(jnp.concatenate([stage[at] for at in range(PANEL // 128)], 1))
        left = jnp.concatenate([high[:, :half], high[:, :half], low[:, :half]], 1)
        return left, jnp.concatenate([high, high, low], 1)

    def inverse_top():
        return jnp.concatenate(
            [inverse_parts[:half, part * PANEL : part * PANEL + half] for part in range(3)], 1
        )

    def column_stages(start, target):
        held = {}

        def cross_half(side):
            scaled, parts, squares = held["points"]
            lanes = slice(side * half, (side + 1) * half)
            inner = jnp.dot(parts, panel_parts[:, lanes], preferred_element_type=F32)
            kernel = jnp.exp(2.0 * inner - squares - panel_rows[0:1, lanes])
            value = (signal_variance * math.sqrt(2.0)) * kernel * (
                scaled[:, -2:-1] - panel_rows[1:2, lanes]
            )
            derivative = value * (math.sqrt(2.0) * (panel_rows[2:3, lanes] - scaled[:, -1:]))
            tiles = range(side * half // 128, (side + 1) * half // 128)
            for at, index in enumerate(tiles):
                tile = cross_next.at[index]
                place = slice(at * 128, (at + 1) * 128)
                tile[pl.ds(0, CHUNK, stride=2), :] = derivative[:, place]
                tile[pl.ds(1, CHUNK, stride=2), :] = value[:, place]
            held[side] = split2(jnp.concatenate([cross_next[index] for index in tiles], 1))

        def place_rows(first, solved):
            count = solved.shape[0]
            high, low = split2(solved)
            target[first : first + count, :] = high
            target[PANEL + first : PANEL + first + count, :] = low
            target[2 * PANEL + first : 2 * PANEL + first + count, :] = high

        def first_stage():
            scaled = cols[:, pl.ds(start, CHUNK)].T
            high, mid = split2(scaled)
            parts = jnp.concatenate([high, high, mid, mid], 1)
            held["points"] = scaled, parts, jnp.sum(scaled * scaled, axis=1, keepdims=True)
            cross_half(0)

        def second_stage():
            cross_half(1)
            high, low = held[0]
            place_rows(0, dot_nt(inverse_top(), jnp.concatenate([high, high, low], 1)))

        def bottom(first):
            high, low = (jnp.concatenate([held[0][k], held[1][k]], 1) for k in range(2))
            parts = jnp.concatenate([high, high, low], 1)
            place_rows(first, dot_nt(inverse_parts[first : first + half // 2, :], parts))

        return [
            first_stage,
            second_stage,
            functools.partial(bottom, half),
            functools.partial(bottom, half + half // 2),
        ]

    @pl.when(step == 0)
    def _():
        scaled = panel[...]
        high, mid = split2(scaled)
        panel_parts[...] = jnp.concatenate([high, mid, high, mid], 0)
        panel_rows[0:1, :] = jnp.sum(scaled * scaled, axis=0, keepdims=True)
        panel_rows[1:2, :] = scaled[-2:-1, :]
        panel_rows[2:3, :] = scaled[-1:, :]
        high, low = split2(inverse[...])
        inverse_parts[...] = jnp.concatenate([high, low, high], 1)
        col = lax.axis_index("pcol")
        first = pl.multiple_of(col * width, width)
        count = cross.shape[1] // 2

        @pl.loop(0, rows.shape[1] // count)
        def _(at):
            start = pl.multiple_of(at * count, count)
            left, parts = cross_parts(rows[:, pl.ds(start, count)], cross)
            solved = jnp.concatenate(
                [dot_nt(left, inverse_top()), dot_nt(parts, inverse_parts[half:, :])], 1
            )
            high, low = split2(solved)
            place = pl.ds(pl.multiple_of(at * 2 * count, 2 * count), 2 * count)
            row_parts[place, :] = jnp.concatenate([high, high, low], 1)
            shard[place, :] = dot_nt(parts, inverse_parts[pl.ds(first, width), :])

        for stage in column_stages(0, even_part):
            stage()

    def subtract(lanes, part, stages):
        quarter = height // len(stages)
        for at, stage in enumerate(stages):
            stage()
            span = slice(at * quarter, (at + 1) * quarter)
            updated[span, lanes] = trailing[span, lanes] - jnp.dot(
                row_parts[span, :], part[...], preferred_element_type=F32
            )

    chunks = cols.shape[1] // CHUNK
    start = pl.multiple_of((2 * step + 1) * CHUNK, CHUNK)
    subtract(slice(0, wide), even_part, column_stages(start, odd_part))
    start = pl.multiple_of(lax.rem(2 * step + 2, chunks) * CHUNK, CHUNK)
    subtract(slice(wide, 2 * wide), odd_part, column_stages(start, even_part))


def update(rows, cols, panel, inverse, trailing, width):
    height, extent = trailing.shape
    variables, count = rows.shape
    tile = 4 * CHUNK
    row_chunk = min(2 * CHUNK, count)
    return pl.pallas_call(
        update_kernel,
        grid=(extent // tile,),
        out_shape=(
            jax.ShapeDtypeStruct((height, extent), F32),
            jax.ShapeDtypeStruct((height, width), F32),
        ),
        in_specs=[
            pl.BlockSpec(rows.shape, lambda j: (0, 0)),
            pl.BlockSpec(cols.shape, lambda j: (0, 0)),
            pl.BlockSpec((variables, PANEL), lambda j: (0, 0)),
            pl.BlockSpec((PANEL, PANEL), lambda j: (0, 0)),
            pl.BlockSpec((height, tile), lambda j: (0, j)),
        ],
        out_specs=(
            pl.BlockSpec((height, tile), lambda j: (0, j)),
            pl.BlockSpec((height, width), lambda j: (0, 0)),
        ),
        scratch_shapes=[
            pltpu.VMEM((4 * variables, PANEL), BF16),
            pltpu.VMEM((8, PANEL), F32),
            pltpu.VMEM((PANEL, 3 * PANEL), BF16),
            pltpu.VMEM((PANEL // 128, 2 * row_chunk, 128), F32),
            pltpu.VMEM((PANEL // 128, 2 * CHUNK, 128), F32),
            pltpu.VMEM((height, 3 * PANEL), BF16),
            pltpu.VMEM((3 * PANEL, 2 * CHUNK), BF16),
            pltpu.VMEM((3 * PANEL, 2 * CHUNK), BF16),
        ],
        compiler_params=pltpu.CompilerParams(vmem_limit_bytes=38 * 2**20),
        name="update_trailing",
    )(rows, cols, panel, inverse, trailing)


def body(designs, length_weights, trailing):
    grid_rows = lax.axis_size("prow")
    grid_cols = lax.axis_size("pcol")
    width = PANEL // grid_cols
    scaled = designs.T * jnp.sqrt(length_weights)[:, None]
    panel, cols = gather_designs(scaled, grid_rows, grid_cols)
    inverse, factor = factor_panel(panel, width)
    updated, shard = update(scaled, cols, panel, inverse, trailing, width)
    return updated, shard, factor


def solution(mesh):
    in_specs = (P("prow", None), P(), P("prow", "pcol"))
    out_specs = (P("prow", "pcol"), P("prow", "pcol"), P(None, "pcol"))
    return jax.shard_map(body, mesh=mesh, in_specs=in_specs, out_specs=out_specs, check_vma=False)
```

```python
import functools
import math

import jax
import jax.numpy as jnp
from jax import lax
from jax.experimental import pallas as pl
from jax.experimental.pallas import tpu as pltpu
from jax.sharding import PartitionSpec as P

PANEL = 512
BLOCK = 128
GROUP = 16
MESH = pl.DeviceIdType.MESH
BF16 = jnp.bfloat16
F32 = jnp.float32
HIGHEST = lax.Precision.HIGHEST

signal_variance = 4.0
nugget_level = 0.1


def split2(x):
    high = x.astype(BF16)
    return high, (x - high.astype(F32)).astype(BF16)


def split3(x):
    high = x.astype(BF16)
    rest = x - high.astype(F32)
    mid = rest.astype(BF16)
    return high, mid, (rest - mid.astype(F32)).astype(BF16)


def dot_tn(a, b, precision=None):
    return lax.dot_general(
        a, b, (((0,), (0,)), ((), ())), precision=precision, preferred_element_type=F32
    )


def dot_nt(a, b):
    return lax.dot_general(a, b, (((1,), (1,)), ((), ())), preferred_element_type=F32)


def gather_kernel(grid_rows, grid_cols, own, panel, cols, send_sem, local_sem, recv_sem):
    me = lax.axis_index("prow")
    col = lax.axis_index("pcol")
    chip, core = me // 2, lax.rem(me, 2)
    rounds = (grid_rows // 2).bit_length() - 1
    per = own.shape[1]
    panel_width = min(per, PANEL)
    holders = PANEL // panel_width
    share = grid_rows // grid_cols
    half = per // 2
    barrier = pltpu.get_barrier_semaphore()
    for step in range(1, grid_rows):
        peer = lax.rem(me + step, grid_rows)
        pl.semaphore_signal(barrier, inc=1, device_id=(peer, col), device_id_type=MESH)
    pl.semaphore_wait(barrier, grid_rows - 1)

    pieces = []
    for at in range(holders):
        source = own.at[:, per - panel_width :]
        target = panel.at[:, at * panel_width : (at + 1) * panel_width]
        pieces.append((grid_rows - holders + at, source, target))
    for part in range(2):
        for at in range(share):
            source = own.at[:, part * half : (part + 1) * half]
            start = at * per + part * half
            pieces.append((col * share + at, source, cols.at[:, start : start + half]))

    sibling = me + 1 - 2 * core
    plans = []
    for at, (holder, source, target) in enumerate(pieces):
        holder_chip, holder_core = holder // 2, lax.rem(holder, 2)
        order = list(range(rounds))
        if at % 2:
            order.reverse()
        differs = [
            lax.rem(chip // 2**bit + holder_chip // 2**bit, 2) == 1 for bit in order
        ]
        peers = [me + (1 - 2 * lax.rem(chip // 2**bit, 2)) * 2 ** (bit + 1) for bit in order]
        same = core == holder_core
        sends = []
        for step in range(rounds):
            wanted = same
            for later in range(step, rounds):
                wanted = wanted & jnp.logical_not(differs[later])
            sends.append((wanted, peers[step], step))
        sends.append((same, sibling, rounds))
        plans.append((at, me == holder, source, target, sends))

    def copy(at, source, target, peer, slot):
        return pltpu.make_async_remote_copy(
            src_ref=source,
            dst_ref=target,
            send_sem=send_sem.at[at, slot],
            recv_sem=recv_sem.at[at],
            device_id=(peer, col),
            device_id_type=MESH,
        )

    for at, holds, source, target, sends in plans:

        @pl.when(holds)
        def _():
            for _, peer, slot in sends:
                copy(at, source, target, peer, slot).start()
            pltpu.make_async_copy(source, target, local_sem.at[at]).start()

    for at, holds, source, target, sends in plans:

        @pl.when(jnp.logical_not(holds))
        def _():
            copy(at, source, target, sibling, 0).wait_recv()
            for wanted, peer, slot in sends:

                @pl.when(wanted)
                def _():
                    copy(at, target, target, peer, slot).start()

    for at, holds, source, target, sends in plans:

        @pl.when(holds)
        def _():
            pltpu.make_async_copy(source, target, local_sem.at[at]).wait()

        for wanted, peer, slot in sends:

            @pl.when(wanted)
            def _():
                copy(at, source, target, peer, slot).wait_send()


def gather_designs(own, grid_rows, grid_cols):
    variables, per = own.shape
    holders = PANEL // min(per, PANEL)
    share = grid_rows // grid_cols
    return pl.pallas_call(
        functools.partial(gather_kernel, grid_rows, grid_cols),
        out_shape=(
            jax.ShapeDtypeStruct((variables, PANEL), F32),
            jax.ShapeDtypeStruct((variables, per * share), F32),
        ),
        in_specs=[pl.BlockSpec(memory_space=pltpu.VMEM)],
        out_specs=(pl.BlockSpec(memory_space=pltpu.VMEM), pl.BlockSpec(memory_space=pltpu.VMEM)),
        scratch_shapes=[
            pltpu.SemaphoreType.DMA((holders + 2 * share, (grid_rows // 2).bit_length())),
            pltpu.SemaphoreType.DMA((holders + 2 * share,)),
            pltpu.SemaphoreType.DMA((holders + 2 * share,)),
        ],
        compiler_params=pltpu.CompilerParams(
            collective_id=0, has_side_effects=True, vmem_limit_bytes=8 * 2**20
        ),
        name="gather_designs",
    )(own)


def factor_block(work):
    row_iota = lax.broadcasted_iota(jnp.int32, (GROUP, BLOCK), 0)
    for first in range(0, BLOCK, GROUP):
        rows = work[first : first + GROUP, :]
        left, right = rows[:, :BLOCK], rows[:, BLOCK:]
        columns = [
            jnp.broadcast_to(left[:, first + k : first + k + 1], (GROUP, BLOCK))
            for k in range(GROUP)
        ]
        scales = jnp.zeros((GROUP, BLOCK), F32)
        for k in range(GROUP):
            root = lax.rsqrt(columns[k][k : k + 1, :])
            inverse = root * root
            scales = jnp.where(row_iota == k, root, scales)
            below = jnp.where(row_iota > k, columns[k], 0.0)
            for m in range(k + 1, GROUP):
                columns[m] = columns[m] - (below * columns[m][k : k + 1, :]) * inverse
            left = left - below * (left[k : k + 1, :] * inverse)
            right = right - below * (right[k : k + 1, :] * inverse)
        left, right = left * scales, right * scales
        work[first : first + GROUP, :BLOCK] = left
        work[first : first + GROUP, BLOCK:] = right
        last = first + GROUP
        if last < BLOCK:
            high, mid, low = split3(jnp.concatenate([left, right], 1))
            a = jnp.concatenate([high, high, mid, high, mid, low], 0)[:, :BLOCK]
            b = jnp.concatenate([high, mid, high, low, mid, high], 0)
            work[last:, :] = work[last:, :] - dot_tn(a, b)[last:, :]


def factor_kernel(panel, inverse, factor, matrix, upper, work):
    width = factor.shape[1]
    scaled = panel[...]
    flipped = scaled.T
    inner = dot_tn(scaled, scaled, HIGHEST)
    squares = jnp.sum(scaled * scaled, axis=0, keepdims=True)
    squares_col = jnp.sum(flipped * flipped, axis=1, keepdims=True)
    kernel = signal_variance * jnp.exp(-(squares_col + squares - 2.0 * inner))
    gap = flipped[:, -2:-1] - scaled[-2:-1, :]
    row_iota = lax.broadcasted_iota(jnp.int32, (PANEL, PANEL), 0)
    col_iota = lax.broadcasted_iota(jnp.int32, (PANEL, PANEL), 1)
    matrix[...] = kernel * (1.0 - 2.0 * gap * gap) + jnp.where(
        row_iota == col_iota, nugget_level, 0.0
    )
    upper[...] = jnp.zeros_like(upper)
    work_row = lax.broadcasted_iota(jnp.int32, (BLOCK, BLOCK), 0)
    work_col = lax.broadcasted_iota(jnp.int32, (BLOCK, BLOCK), 1)
    identity = jnp.where(work_row == work_col, 1.0, 0.0)
    blocks = PANEL // BLOCK

    @pl.loop(0, blocks)
    def _(at):
        offset = pl.multiple_of(at * BLOCK, BLOCK)
        work[:, :BLOCK] = matrix[pl.ds(offset, BLOCK), pl.ds(offset, BLOCK)]
        work[:, BLOCK:] = identity
        factor_block(work)
        part_upper = jnp.where(work_col >= work_row, work[:, :BLOCK], 0.0)
        part_inverse = jnp.where(work_col <= work_row, work[:, BLOCK:], 0.0)
        for k in range(blocks):

            @pl.when(at == k)
            def _():
                low, high = k * BLOCK, (k + 1) * BLOCK
                solved = jnp.dot(
                    part_inverse,
                    matrix[low:high, :],
                    precision=HIGHEST,
                    preferred_element_type=F32,
                )
                pieces = [part_inverse]
                if k > 0:
                    pieces.insert(0, solved[:, :low])
                if high < PANEL:
                    pieces.append(solved[:, high:])
                    upper[low:high, high:] = solved[:, high:]
                upper[low:high, low:high] = part_upper
                whole = jnp.concatenate(pieces, 1)
                matrix[low:high, :] = whole
                if high < PANEL:
                    matrix[high:, low:high] = jnp.zeros((PANEL - high, BLOCK), F32)
                    matrix[high:, :] = matrix[high:, :] - dot_tn(
                        solved[:, high:], whole, HIGHEST
                    )

    inverse[...] = jnp.where(col_iota <= row_iota, matrix[...], 0.0)
    col = lax.axis_index("pcol")
    first = pl.multiple_of(col * width, width)
    factor[...] = upper[pl.ds(first, width), :].T


def factor_panel(panel, width):
    return pl.pallas_call(
        factor_kernel,
        out_shape=(
            jax.ShapeDtypeStruct((PANEL, PANEL), F32),
            jax.ShapeDtypeStruct((PANEL, width), F32),
        ),
        in_specs=[pl.BlockSpec(memory_space=pltpu.VMEM)],
        out_specs=(pl.BlockSpec(memory_space=pltpu.VMEM), pl.BlockSpec(memory_space=pltpu.VMEM)),
        scratch_shapes=[
            pltpu.VMEM((PANEL, PANEL), F32),
            pltpu.VMEM((PANEL, PANEL), F32),
            pltpu.VMEM((BLOCK, 2 * BLOCK), F32),
        ],
        compiler_params=pltpu.CompilerParams(vmem_limit_bytes=16 * 2**20),
        name="factor_panel",
    )(panel)


CHUNK = 128


def update_kernel(
    rows, cols, panel, inverse, trailing,
    updated, shard,
    panel_parts, panel_rows, inverse_parts, cross, cross_next, row_parts, even_part, odd_part,
):
    step = pl.program_id(0)
    width = shard.shape[1]
    height = trailing.shape[0]
    half = PANEL // 2
    wide = 2 * CHUNK

    def cross_parts(points, stage):
        count = points.shape[1]
        scaled = points.T
        high, mid = split2(scaled)
        parts = jnp.concatenate([high, high, mid, mid], 1)
        inner = jnp.dot(parts, panel_parts[...], preferred_element_type=F32)
        squares = jnp.sum(scaled * scaled, axis=1, keepdims=True)
        kernel = jnp.exp(2.0 * inner - squares - panel_rows[0:1, :])
        value = (signal_variance * math.sqrt(2.0)) * kernel * (
            scaled[:, -2:-1] - panel_rows[1:2, :]
        )
        derivative = value * (math.sqrt(2.0) * (panel_rows[2:3, :] - scaled[:, -1:]))
        for lane in range(0, PANEL, 128):
            tile = stage.at[lane // 128]
            tile[pl.ds(0, count, stride=2), :] = derivative[:, lane : lane + 128]
            tile[pl.ds(1, count, stride=2), :] = value[:, lane : lane + 128]
        high, low = split2(jnp.concatenate([stage[at] for at in range(PANEL // 128)], 1))
        left = jnp.concatenate([high[:, :half], high[:, :half], low[:, :half]], 1)
        return left, jnp.concatenate([high, high, low], 1)

    def inverse_top():
        return jnp.concatenate(
            [inverse_parts[:half, part * PANEL : part * PANEL + half] for part in range(3)], 1
        )

    def make_columns(start, target):
        left, parts = cross_parts(cols[:, pl.ds(start, CHUNK)], cross_next)
        solved = jnp.concatenate(
            [dot_nt(inverse_top(), left), dot_nt(inverse_parts[half:, :], parts)], 0
        )
        high, low = split2(solved)
        target[:PANEL, :] = high
        target[PANEL : 2 * PANEL, :] = low
        target[2 * PANEL :, :] = high

    @pl.when(step == 0)
    def _():
        scaled = panel[...]
        high, mid = split2(scaled)
        panel_parts[...] = jnp.concatenate([high, mid, high, mid], 0)
        panel_rows[0:1, :] = jnp.sum(scaled * scaled, axis=0, keepdims=True)
        panel_rows[1:2, :] = scaled[-2:-1, :]
        panel_rows[2:3, :] = scaled[-1:, :]
        high, low = split2(inverse[...])
        inverse_parts[...] = jnp.concatenate([high, low, high], 1)
        col = lax.axis_index("pcol")
        first = pl.multiple_of(col * width, width)
        count = cross.shape[1] // 2

        @pl.loop(0, rows.shape[1] // count)
        def _(at):
            start = pl.multiple_of(at * count, count)
            left, parts = cross_parts(rows[:, pl.ds(start, count)], cross)
            solved = jnp.concatenate(
                [dot_nt(left, inverse_top()), dot_nt(parts, inverse_parts[half:, :])], 1
            )
            high, low = split2(solved)
            place = pl.ds(pl.multiple_of(at * 2 * count, 2 * count), 2 * count)
            row_parts[place, :] = jnp.concatenate([high, high, low], 1)
            shard[place, :] = dot_nt(parts, inverse_parts[pl.ds(first, width), :])

        make_columns(0, even_part)

    def subtract(lanes, part):
        for at in range(0, height, 512):
            updated[at : at + 512, lanes] = trailing[at : at + 512, lanes] - jnp.dot(
                row_parts[at : at + 512, :], part[...], preferred_element_type=F32
            )

    chunks = cols.shape[1] // CHUNK
    make_columns(pl.multiple_of((2 * step + 1) * CHUNK, CHUNK), odd_part)
    subtract(slice(0, wide), even_part)
    following = lax.rem(2 * step + 2, chunks)
    make_columns(pl.multiple_of(following * CHUNK, CHUNK), even_part)
    subtract(slice(wide, 2 * wide), odd_part)


def update(rows, cols, panel, inverse, trailing, width):
    height, extent = trailing.shape
    variables, count = rows.shape
    tile = 4 * CHUNK
    row_chunk = min(2 * CHUNK, count)
    return pl.pallas_call(
        update_kernel,
        grid=(extent // tile,),
        out_shape=(
            jax.ShapeDtypeStruct((height, extent), F32),
            jax.ShapeDtypeStruct((height, width), F32),
        ),
        in_specs=[
            pl.BlockSpec(rows.shape, lambda j: (0, 0)),
            pl.BlockSpec(cols.shape, lambda j: (0, 0)),
            pl.BlockSpec((variables, PANEL), lambda j: (0, 0)),
            pl.BlockSpec((PANEL, PANEL), lambda j: (0, 0)),
            pl.BlockSpec((height, tile), lambda j: (0, j)),
        ],
        out_specs=(
            pl.BlockSpec((height, tile), lambda j: (0, j)),
            pl.BlockSpec((height, width), lambda j: (0, 0)),
        ),
        scratch_shapes=[
            pltpu.VMEM((4 * variables, PANEL), BF16),
            pltpu.VMEM((8, PANEL), F32),
            pltpu.VMEM((PANEL, 3 * PANEL), BF16),
            pltpu.VMEM((PANEL // 128, 2 * row_chunk, 128), F32),
            pltpu.VMEM((PANEL // 128, 2 * CHUNK, 128), F32),
            pltpu.VMEM((height, 3 * PANEL), BF16),
            pltpu.VMEM((3 * PANEL, 2 * CHUNK), BF16),
            pltpu.VMEM((3 * PANEL, 2 * CHUNK), BF16),
        ],
        compiler_params=pltpu.CompilerParams(vmem_limit_bytes=44 * 2**20),
        name="update_trailing",
    )(rows, cols, panel, inverse, trailing)


def body(designs, length_weights, trailing):
    grid_rows = lax.axis_size("prow")
    grid_cols = lax.axis_size("pcol")
    width = PANEL // grid_cols
    scaled = designs.T * jnp.sqrt(length_weights)[:, None]
    panel, cols = gather_designs(scaled, grid_rows, grid_cols)
    inverse, factor = factor_panel(panel, width)
    updated, shard = update(scaled, cols, panel, inverse, trailing, width)
    return updated, shard, factor


def solution(mesh):
    in_specs = (P("prow", None), P(), P("prow", "pcol"))
    out_specs = (P("prow", "pcol"), P("prow", "pcol"), P(None, "pcol"))
    return jax.shard_map(body, mesh=mesh, in_specs=in_specs, out_specs=out_specs, check_vma=False)
```
